32 devices in a mesh: fsdp: 8 (over z, x), seq: 4 (over y, core).
Axes of the slice: x: 2, y: 2, z: 4, core: 2. Of those that a mesh axis runs over, the one named last changes fastest.
Arguments:
- tokens: bfloat16 [24, 1024, 1024], P('fsdp', 'seq'), may hold values from -6 to 6
- segments: int32 [24, 1024], P('fsdp', 'seq'), may hold values from 0 to 1023, as said below
- qkv_weight: bfloat16 [1024, 3072], P('fsdp'), may hold values from -0.1875 to 0.1875
- query_bias: bfloat16 [1024], P('fsdp'), may hold values from -3 to 3
- value_bias: bfloat16 [1024], P('fsdp'), may hold values from -3 to 3
- out_weight: bfloat16 [1024, 1024], P('fsdp'), may hold values from -1.5 to 1.5
- out_bias: bfloat16 [1024], P('fsdp'), may hold values from -3 to 3
- first_gain: bfloat16 [1024], P('fsdp'), may hold values from 0.5 to 1.5
- first_shift: bfloat16 [1024], P('fsdp'), may hold values from -3 to 3
- hidden_weight: bfloat16 [1024, 4096], P('fsdp'), may hold values from -0.1875 to 0.1875
- hidden_bias: bfloat16 [4096], P('fsdp'), may hold values from -3 to 3
- down_weight: bfloat16 [4096, 1024], P('fsdp'), may hold values from -0.09375 to 0.09375
- down_bias: bfloat16 [1024], P('fsdp'), may hold values from -3 to 3
- second_gain: bfloat16 [1024], P('fsdp'), may hold values from 0.5 to 1.5
- second_shift: bfloat16 [1024], P('fsdp'), may hold values from -3 to 3
- cotangent: bfloat16 [24, 1024, 1024], P('fsdp', 'seq'), may hold values from -6 to 6
Outputs:
- block_out: bfloat16 [24, 1024, 1024], P('fsdp', 'seq')
- grad_tokens: float32 [24, 1024, 1024], P('fsdp', 'seq')
- grad_qkv_weight: float32 [1024, 3072], P('fsdp')
- grad_query_bias: float32 [1024], P('fsdp')
- grad_value_bias: float32 [1024], P('fsdp')
- grad_out_weight: float32 [1024, 1024], P('fsdp')
- grad_out_bias: float32 [1024], P('fsdp')
- grad_first_gain: float32 [1024], P('fsdp')
- grad_first_shift: float32 [1024], P('fsdp')
- grad_hidden_weight: float32 [1024, 4096], P('fsdp')
- grad_hidden_bias: float32 [4096], P('fsdp')
- grad_down_weight: float32 [4096, 1024], P('fsdp')
- grad_down_bias: float32 [1024], P('fsdp')
- grad_second_gain: float32 [1024], P('fsdp')
- grad_second_shift: float32 [1024], P('fsdp')
The draws below stay inside these ranges and needn't reach their ends.
Inputs may be any that keep to these rules, and one draw needn't show every extreme that they name: `segments`: A token's segment number is the position within its sequence of its document's first token, so it never falls along a sequence. On each index of fsdp one of its 3 sequences is a single document; every other sequence ends with a document of one token.
All inputs are finite; a program needn't handle non-finite values.
Results may differ from the reference program's by a relative error of at most 0.017.
Values may be sent and summed in bfloat16 or wider, within the bound.
A program may use at most 256 MiB of HBM per device.

```python
import jax
import jax.numpy as jnp
from jax import lax

D = 1024
H = 16
DH = 64
FF = 4096
BLK = 256
SEQS_DEV = 3
LEN = 1024
SEQS = 24


def draw_segments(key, part):
    key = jax.random.fold_in(key, 11)
    cut_key, whole_key = jax.random.split(key)
    places = jnp.arange(LEN, dtype=jnp.int32)[None, :]
    cuts = jax.random.randint(cut_key, (SEQS, LEN), 0, BLK) == 0
    cuts = cuts | (places == LEN - 1)
    starts = jnp.where(cuts, places, 0)
    firsts = lax.cummax(starts, axis=1)
    chosen = jax.random.randint(whole_key, (SEQS // SEQS_DEV, 1), 0, SEQS_DEV)
    members = jnp.arange(SEQS_DEV, dtype=jnp.int32)[None, :]
    single = (members == chosen).reshape(SEQS, 1)
    return jnp.where(single, 0, firsts).astype(jnp.int32)


def raised(drawn, stream_key, source, target, blocks, factor):
    def block_of(dim):
        return (jnp.arange(drawn.shape[dim]) // (drawn.shape[dim] // blocks)).reshape((-1,) + (1,) * (drawn.ndim - 1 - dim))

    near = jax.random.permutation(stream_key, blocks)[block_of(target)]
    second = (block_of(target) + blocks // 2) % blocks
    return jnp.where((block_of(source) == near) | (block_of(source) == second), factor * drawn, drawn)


def shard_levels(stream_key, shape, pieces, least, top_value):
    def one(dim, blocks):
        heights = jax.random.uniform(jax.random.fold_in(jax.random.fold_in(stream_key, 6), dim), (blocks,), jnp.float32, least / len(pieces), top_value / len(pieces))
        return jnp.repeat(jnp.exp(heights), shape[dim] // blocks).reshape((-1,) + (1,) * (len(shape) - dim - 1))

    loudness = one(*pieces[0])
    for cut in pieces[1:]:
        loudness = loudness * one(*cut)
    return loudness


def bell_draw(own_key, extent, spread, reach, pieces=(), kind=jnp.bfloat16):
    array = spread * jax.random.normal(own_key, extent, jnp.float32)
    if pieces:
        array = array * shard_levels(own_key, extent, pieces, -0.22, 0.18)
    return jnp.clip(array, -reach, reach).astype(kind)


def noise_with(rng, shape, spread, most, pieces, heavy, kind=jnp.bfloat16):
    array = spread * jax.random.normal(rng, shape, jnp.float32)
    if pieces:
        array = array * shard_levels(rng, shape, pieces, -0.22, 0.18)
    return jnp.clip(raised(array, jax.random.fold_in(rng, 3), *heavy), -most, most).astype(kind)


def setup_inputs(seed: int = 0) -> dict:
    streams_of = jax.random.split(jax.random.key(seed), 17)
    tokens = bell_draw(streams_of[0], (SEQS, LEN, D), 1.0, 6.0, ((0, 8), (1, 4)))
    segments = draw_segments(jax.random.fold_in(streams_of[16], 71), 0)
    qkv_weight = bell_draw(streams_of[2], (D, 3 * D), D ** -0.5, 0.1875, ((0, 8),))
    query_bias = bell_draw(streams_of[3], (D,), 0.5, 3.0, ((0, 8),))
    value_bias = bell_draw(streams_of[4], (D,), 0.5, 3.0, ((0, 8),))
    out_weight = bell_draw(streams_of[5], (D, D), (D // 64) ** -0.5, 1.5, ((0, 8),))
    out_bias = bell_draw(streams_of[6], (D,), 0.5, 3.0, ((0, 8),))
    first_gain = jnp.clip(1.0 + 0.1 * jax.random.normal(streams_of[7], (D,), jnp.float32), 0.5, 1.5).astype(jnp.bfloat16)
    first_shift = bell_draw(streams_of[8], (D,), 0.5, 3.0, ((0, 8),))
    hidden_weight = bell_draw(streams_of[9], (D, FF), D ** -0.5, 0.1875, ((0, 8),))
    hidden_bias = bell_draw(streams_of[10], (FF,), 0.5, 3.0, ((0, 8),))
    down_weight = bell_draw(streams_of[11], (FF, D), FF ** -0.5, 0.09375, ((0, 8),))
    down_bias = bell_draw(streams_of[12], (D,), 0.5, 3.0, ((0, 8),))
    second_gain = jnp.clip(1.0 + 0.1 * jax.random.normal(streams_of[13], (D,), jnp.float32), 0.5, 1.5).astype(jnp.bfloat16)
    second_shift = bell_draw(streams_of[14], (D,), 0.5, 3.0, ((0, 8),))
    cotangent = noise_with(streams_of[15], (SEQS, LEN, D), 1.0, 6.0, ((0, 8), (1, 4)), (0, 2, 8, 2.0))
    return {"tokens": tokens, "segments": segments, "qkv_weight": qkv_weight, "query_bias": query_bias, "value_bias": value_bias, "out_weight": out_weight, "out_bias": out_bias, "first_gain": first_gain, "first_shift": first_shift, "hidden_weight": hidden_weight, "hidden_bias": hidden_bias, "down_weight": down_weight, "down_bias": down_bias, "second_gain": second_gain, "second_shift": second_shift, "cotangent": cotangent}


norm_epsilon = 1e-05
masked_score = -1e+30
highest = lax.Precision.HIGHEST

@jax.custom_vjp
def low(v):
    return lax.optimization_barrier(v.astype(jnp.bfloat16)).astype(jnp.float32)

@jax.custom_vjp
def low_back(v):
    return v

def low_keep(v):
    return (low(v), None)

def low_pass(kept, grad):
    return (grad,)

def back_keep(v):
    return (v, None)

def back_low(kept, grad):
    return (low(grad),)
low.defvjp(low_keep, low_pass)
low_back.defvjp(back_keep, back_low)

def layer_norm(values, gain, shift):
    row_mean = lax.optimization_barrier(jnp.mean(values, -1, keepdims=True))
    centered = values - row_mean
    variance = lax.optimization_barrier(jnp.mean(centered * centered, -1, keepdims=True))
    return centered * lax.rsqrt(variance + norm_epsilon) * gain + shift

def project(inputs, weight):
    return jnp.einsum('gtd,de->gte', inputs, weight, precision=highest)

def attend(scanned):
    queries, key_rows, value_rows, segment_ids = scanned
    scores = jnp.einsum('qhe,khe->hqk', queries, key_rows, precision=highest) * DH ** (-0.5)
    scores = low_back(scores)
    allowed = (segment_ids[:, None] == segment_ids[None, :])[None]
    scores = jnp.where(allowed, scores, masked_score)
    softmax_weights = low(jax.nn.softmax(scores, axis=-1))
    return jnp.einsum('hqk,khe->qhe', softmax_weights, value_rows, precision=highest)

def forward(inputs, parameters, segment_ids):
    qkv_weight, query_bias, value_bias, out_weight, out_bias, first_gain, first_shift, hidden_weight, hidden_bias, down_weight, down_bias, second_gain, second_shift = parameters
    projected = project(inputs, qkv_weight)
    queries = low(low_back(projected[..., :D] + query_bias))
    key_rows = low(low_back(projected[..., D:2 * D]))
    value_rows = low(low_back(projected[..., 2 * D:] + value_bias))
    head_shape = (inputs.shape[0], LEN, H, DH)
    context = lax.map(jax.checkpoint(attend), (queries.reshape(head_shape), key_rows.reshape(head_shape), value_rows.reshape(head_shape), segment_ids))
    context = low(low_back(context.reshape(inputs.shape)))
    attention = low_back(project(context, out_weight) + out_bias)
    hidden = layer_norm(inputs + attention, first_gain, first_shift)
    preactivation = low_back(project(low(hidden), hidden_weight) + hidden_bias)
    activation = low(jax.nn.gelu(preactivation, approximate=False))
    branch = low_back(project(activation, down_weight) + down_bias)
    return layer_norm(hidden + branch, second_gain, second_shift)

def reference(tokens, segments, qkv_weight, query_bias, value_bias, out_weight, out_bias, first_gain, first_shift, hidden_weight, hidden_bias, down_weight, down_bias, second_gain, second_shift, cotangent):
    parameters = tuple((weight.astype(jnp.float32) for weight in (qkv_weight, query_bias, value_bias, out_weight, out_bias, first_gain, first_shift, hidden_weight, hidden_bias, down_weight, down_bias, second_gain, second_shift)))
    group_count = SEQS // SEQS_DEV
    inputs = tokens.astype(jnp.float32).reshape(group_count, SEQS_DEV, LEN, D)
    cotangents = cotangent.astype(jnp.float32).reshape(group_count, SEQS_DEV, LEN, D)
    segment_ids = segments.reshape(group_count, SEQS_DEV, LEN)

    def accumulate(totals, scanned):
        inputs_group, group_ids, gradient_in = scanned
        result, pullback = jax.vjp(lambda values, weights: forward(values, weights, group_ids), inputs_group, parameters)
        grad_inputs, grad_weights = pullback(gradient_in)
        totals = tuple((running + fresh for running, fresh in zip(totals, grad_weights)))
        return (totals, (result.astype(jnp.bfloat16), grad_inputs))
    initial = tuple((jnp.zeros(weight.shape, jnp.float32) for weight in parameters))
    totals, (outputs, grad_inputs) = lax.scan(accumulate, initial, (inputs, segment_ids, cotangents))
    return (outputs.reshape(SEQS, LEN, D), grad_inputs.reshape(SEQS, LEN, D), totals[0], totals[1], totals[2], totals[3], totals[4], totals[5], totals[6], totals[7], totals[8], totals[9], totals[10], totals[11], totals[12])
```

```python
import math

import jax
import jax.numpy as jnp
from jax import lax
from jax.experimental import pallas as pl
from jax.experimental.pallas import tpu as pltpu
from jax.sharding import PartitionSpec as P

DH = 64
QBLK = 256
norm_epsilon = 1e-05
masked_score = -1e30
F32 = jnp.float32
BF16 = jnp.bfloat16
NT = (((1,), (1,)), ((), ()))
TN = (((0,), (0,)), ((), ()))
NN = (((1,), (0,)), ((), ()))


def dot(a, b, dims=NN):
    return lax.dot_general(a, b, dims, preferred_element_type=F32)


def attend_kernel(q_ref, k_ref, v_ref, seg_col, seg_row, o_ref, lse_ref):
    heads = q_ref.shape[1] // DH
    allowed = seg_col[...] == seg_row[...]
    for h in range(heads):
        cols = slice(h * DH, (h + 1) * DH)
        scores = dot(k_ref[:, cols], q_ref[:, cols], NT)
        scores = jnp.where(allowed, scores, masked_score)
        peak = jnp.max(scores, axis=0, keepdims=True)
        raw = jnp.exp(scores - peak)
        total = jnp.sum(raw, axis=0, keepdims=True)
        part = dot(v_ref[:, cols], raw.astype(BF16), TN) / total
        o_ref[:, cols] = part.T.astype(BF16)
        lse_ref[h : h + 1, :] = peak + jnp.log(total)


def attend(qkv, seg_col, seg_row):
    length, width = qkv.shape[0], qkv.shape[1] // 3
    heads = width // DH
    return pl.pallas_call(
        attend_kernel,
        grid=(length // QBLK,),
        in_specs=[
            pl.BlockSpec((QBLK, width), lambda i: (i, 0)),
            pl.BlockSpec((length, width), lambda i: (0, 1)),
            pl.BlockSpec((length, width), lambda i: (0, 2)),
            pl.BlockSpec((length, 1), lambda i: (0, 0)),
            pl.BlockSpec((1, QBLK), lambda i: (0, i)),
        ],
        out_specs=[
            pl.BlockSpec((QBLK, width), lambda i: (i, 0)),
            pl.BlockSpec((heads, QBLK), lambda i: (0, i)),
        ],
        out_shape=[
            jax.ShapeDtypeStruct((length, width), BF16),
            jax.ShapeDtypeStruct((heads, length), F32),
        ],
        compiler_params=pltpu.CompilerParams(vmem_limit_bytes=40 * 2**20),
        cost_estimate=pl.CostEstimate(
            flops=16 * heads * length * length * DH,
            bytes_accessed=8 * length * width,
            transcendentals=heads * length * length,
        ),
    )(qkv, qkv, qkv, seg_col, seg_row)


def back_kernel(q_ref, k_ref, v_ref, do_ref, lse_ref, seg_col, seg_row, out_ref, dk_acc, dv_acc):
    step = pl.program_id(0)
    width = q_ref.shape[1]
    heads = width // DH

    @pl.when(step == 0)
    def _():
        dk_acc[...] = jnp.zeros_like(dk_acc)
        dv_acc[...] = jnp.zeros_like(dv_acc)

    allowed = seg_col[...] == seg_row[...]
    rows = pl.ds(pl.multiple_of(step * QBLK, QBLK), QBLK)
    for h in range(heads):
        cols = slice(h * DH, (h + 1) * DH)
        queries, keys, grads = q_ref[:, cols], k_ref[:, cols], do_ref[:, cols]
        scores = dot(keys, queries, NT)
        soft = jnp.exp(jnp.where(allowed, scores, masked_score) - lse_ref[h : h + 1, :])
        grad_soft = dot(v_ref[:, cols], grads, NT)
        inner = jnp.sum(soft * grad_soft, axis=0, keepdims=True)
        grad_scores = (soft * (grad_soft - inner)).astype(BF16)
        dk_acc[:, cols] += dot(grad_scores, queries)
        dv_acc[:, cols] += dot(soft.astype(BF16), grads)
        grad_query = dot(keys, grad_scores, TN) * DH ** (-0.5)
        out_ref[rows, cols] = grad_query.T.astype(BF16)

    @pl.when(step == pl.num_programs(0) - 1)
    def _():
        out_ref[:, width : 2 * width] = dk_acc[...].astype(BF16)
        out_ref[:, 2 * width :] = dv_acc[...].astype(BF16)


def attend_back(qkv, grad_context, lse, seg_col, seg_row):
    length, width = qkv.shape[0], qkv.shape[1] // 3
    heads = width // DH
    return pl.pallas_call(
        back_kernel,
        grid=(length // QBLK,),
        in_specs=[
            pl.BlockSpec((QBLK, width), lambda i: (i, 0)),
            pl.BlockSpec((length, width), lambda i: (0, 1)),
            pl.BlockSpec((length, width), lambda i: (0, 2)),
            pl.BlockSpec((QBLK, width), lambda i: (i, 0)),
            pl.BlockSpec((heads, QBLK), lambda i: (0, i)),
            pl.BlockSpec((length, 1), lambda i: (0, 0)),
            pl.BlockSpec((1, QBLK), lambda i: (0, i)),
        ],
        out_specs=pl.BlockSpec((length, 3 * width), lambda i: (0, 0)),
        out_shape=jax.ShapeDtypeStruct((length, 3 * width), BF16),
        scratch_shapes=[pltpu.VMEM((length, width), F32), pltpu.VMEM((length, width), F32)],
        compiler_params=pltpu.CompilerParams(vmem_limit_bytes=40 * 2**20),
        cost_estimate=pl.CostEstimate(
            flops=40 * heads * length * length * DH,
            bytes_accessed=14 * length * width,
            transcendentals=heads * length * length,
        ),
    )(qkv, qkv, qkv, grad_context, lse, seg_col, seg_row)


def norm_rows(values):
    row_mean = jnp.mean(values, -1, keepdims=True)
    centered = values - row_mean
    inverse = lax.rsqrt(jnp.mean(centered * centered, -1, keepdims=True) + norm_epsilon)
    return centered * inverse, inverse


def norm_back(upstream, normed, inverse, gain):
    scaled = upstream * gain
    first_mean = jnp.mean(scaled, -1, keepdims=True)
    second_mean = jnp.mean(scaled * normed, -1, keepdims=True)
    return inverse * (scaled - first_mean - normed * second_mean)


def make_body(n, k):
    def swap(array, flip):
        return lax.ppermute(array, "seq", [(i, i ^ flip) for i in range(k)])

    def gather(own):
        near = swap(own, 1)
        far = swap(own, 2)
        return jnp.concatenate([own, near, far, swap(far, 1)], axis=0)

    def scatter(partial):
        rows = partial.shape[0] // k
        low = partial.astype(BF16)
        block = lambda j: low[j * rows : (j + 1) * rows]
        got = swap(jnp.concatenate([block(1), block(3)], axis=0), 1)
        exact = lambda j: partial[j * rows : (j + 1) * rows]
        other = swap((exact(2) + got[rows:].astype(F32)).astype(BF16), 2)
        return exact(0) + got[:rows].astype(F32) + other.astype(F32)

    def exchange(blocks):
        me = lax.axis_index("seq")
        return [blocks(me)] + [swap(blocks(me ^ d), d) for d in range(1, k)]

    def absolute(pieces):
        me = lax.axis_index("seq")
        stacked = jnp.stack(pieces)
        return [lax.dynamic_index_in_dim(stacked, me ^ t, 0, keepdims=False) for t in range(k)]

    def body(
        tokens,
        segments,
        qkv_weight,
        query_bias,
        value_bias,
        out_weight,
        out_bias,
        first_gain,
        first_shift,
        hidden_weight,
        hidden_bias,
        down_weight,
        down_bias,
        second_gain,
        second_shift,
        cotangent,
    ):
        me = lax.axis_index("seq")
        seqs, blk, D = tokens.shape
        FF = hidden_weight.shape[1]
        wide = D // k
        units = FF // k
        shard = D // n
        unit_shard = units // n

        small = jnp.concatenate(
            [
                query_bias,
                value_bias,
                out_bias,
                first_gain,
                first_shift,
                down_bias,
                second_gain,
                second_shift,
                hidden_bias,
            ]
        )
        count = small.shape[0]
        extra = 16
        small = jnp.pad(small, (0, extra * 3 * wide - count)).reshape(extra, 3 * wide)
        mine = lax.dynamic_index_in_dim(
            qkv_weight.reshape(shard, 3, k, wide), me, 2, keepdims=False
        ).reshape(shard, 3 * wide)
        packed = lax.all_gather(jnp.concatenate([mine, small], axis=0), "fsdp", axis=0)
        w_qkv = packed[:, :shard].reshape(D, 3 * wide)
        vectors = packed[:, shard:].reshape(n, extra * 3 * wide)[:, :count].astype(F32)
        vector = lambda j: vectors[:, j * shard : (j + 1) * shard].reshape(1, D)
        (qbias, vbias, obias, gain_one, shift_one, dbias, gain_two, shift_two) = [
            vector(j) for j in range(8)
        ]
        hbias = lax.dynamic_index_in_dim(
            vectors[:, 8 * shard :].reshape(n, k, unit_shard), me, 1, keepdims=False
        ).reshape(1, units)
        own_columns = lambda v: lax.dynamic_slice_in_dim(v, me * wide, wide, 1)
        qkv_bias = jnp.concatenate(
            [own_columns(qbias), jnp.zeros((1, wide), F32), own_columns(vbias)], axis=1
        )
        qkv_scale = jnp.concatenate(
            [jnp.full((1, wide), DH ** (-0.5), F32), jnp.ones((1, 2 * wide), F32)], axis=1
        )

        out_mine = lax.dynamic_slice_in_dim(out_weight, me * wide, wide, 1)
        out_columns = lax.all_gather(out_mine, "fsdp", axis=0, tiled=True)
        w_out = jnp.concatenate(
            absolute(exchange(lambda t: lax.dynamic_slice_in_dim(out_columns, t * wide, wide, 0))),
            axis=1,
        )
        up_mine = lax.dynamic_index_in_dim(
            hidden_weight.reshape(shard, n, k, unit_shard), me, 2, keepdims=False
        ).reshape(shard, units)
        w_up = lax.all_gather(up_mine, "fsdp", axis=0, tiled=True)
        down_mine = lax.dynamic_slice_in_dim(down_weight, me * unit_shard, unit_shard, 0)
        w_down = lax.all_gather(down_mine, "fsdp", axis=0, tiled=True)

        seg_all = jnp.concatenate(
            [segments, swap(segments, 1), swap(segments, 2), swap(segments, 3)], axis=1
        )

        state = []
        for i in range(seqs):
            x = gather(tokens[i])
            seg_col, seg_row = seg_all[i][:, None], seg_all[i][None, :]
            qkv = ((dot(x, w_qkv) + qkv_bias) * qkv_scale).astype(BF16)
            context, lse = attend(qkv, seg_col, seg_row)
            state.append([x, seg_col, seg_row, qkv, context, lse, scatter(dot(context, w_out))])
        for i in range(seqs):
            attention = state[i][-1] + obias
            normed_one, inverse_one = norm_rows(tokens[i].astype(F32) + attention)
            hidden = normed_one * gain_one + shift_one
            hid = gather(hidden.astype(BF16))
            pre = dot(hid, w_up) + hbias
            cdf = 0.5 * (1.0 + lax.erf(pre * math.sqrt(0.5)))
            act = (pre * cdf).astype(BF16)
            slope = (cdf + pre * (jnp.exp(-0.5 * pre * pre) / math.sqrt(2 * math.pi))).astype(BF16)
            branch = scatter(dot(act, w_down))
            state[i] += [normed_one, inverse_one, hidden, hid, act, slope, branch]

        outs, grad_tokens = [], []
        sums = [0.0] * 6
        g_down = g_up = g_out = g_qkv = 0.0
        s_pre = s_qkv = 0.0
        grads = []
        total = lambda a: jnp.sum(a, axis=0)
        for i in range(seqs):
            normed_one, inverse_one, hidden, hid, act, slope, branch = state[i][7:]
            normed_two, inverse_two = norm_rows(hidden + branch + dbias)
            outs.append((normed_two * gain_two + shift_two).astype(BF16))
            upstream = cotangent[i].astype(F32)
            grad_two = norm_back(upstream, normed_two, inverse_two, gain_two)
            grad_branch = grad_two.astype(BF16)
            sums[3] += total(grad_branch.astype(F32))
            sums[4] += total(upstream * normed_two)
            sums[5] += total(upstream)
            gb = gather(grad_branch)
            g_down += dot(act, gb, TN)
            grad_pre = (dot(gb, w_down, NT) * slope.astype(F32)).astype(BF16)
            s_pre += total(grad_pre.astype(F32))
            g_up += dot(hid, grad_pre, TN)
            grad_hidden = grad_two + scatter(dot(grad_pre, w_up, NT))
            grads.append(grad_hidden)

        def shared(grad):
            return lax.psum_scatter(grad.astype(BF16), "fsdp", scatter_dimension=0, tiled=True)

        r_down = shared(g_down)
        r_up = shared(g_up)

        for i in range(seqs):
            x, seg_col, seg_row, qkv, context, lse = state[i][:6]
            normed_one, inverse_one = state[i][7:9]
            grad_hidden = grads[i]
            grad_one = norm_back(grad_hidden, normed_one, inverse_one, gain_one)
            grad_attention = grad_one.astype(BF16)
            sums[0] += total(grad_attention.astype(F32))
            sums[1] += total(grad_hidden * normed_one)
            sums[2] += total(grad_hidden)
            ga = gather(grad_attention)
            g_out += dot(context, ga, TN)
            grad_context = dot(ga, w_out, NT).astype(BF16)
            dqkv = attend_back(qkv, grad_context, lse, seg_col, seg_row)
            s_qkv += total(dqkv.astype(F32))
            g_qkv += dot(x, dqkv, TN)
            grad_tokens.append(grad_one + scatter(dot(dqkv, w_qkv, NT)))

        g_out = g_out.astype(BF16)
        r_out = shared(
            jnp.concatenate(
                absolute(exchange(lambda t: lax.dynamic_slice_in_dim(g_out, t * wide, wide, 1))),
                axis=0,
            )
        )

        place = lambda v: lax.dynamic_update_slice_in_dim(
            jnp.zeros((D,), F32), v, me * wide, 0
        )
        full = [place(s_qkv[:wide]), place(s_qkv[2 * wide :])] + sums
        hidden_sum = lax.dynamic_update_slice_in_dim(
            jnp.zeros((n, k, unit_shard), F32), s_pre.reshape(n, 1, unit_shard), me, 1
        ).reshape(n, k * unit_shard)
        vector_sums = jnp.concatenate([v.reshape(n, shard) for v in full] + [hidden_sum], axis=1)
        vector_sums = jnp.pad(vector_sums, ((0, 0), (0, extra * 3 * wide - count)))
        joined = jnp.concatenate(
            [
                g_qkv.astype(BF16).reshape(n, shard, 3 * wide),
                vector_sums.astype(BF16).reshape(n, extra, 3 * wide),
            ],
            axis=1,
        )
        r_qkv = lax.psum_scatter(joined, "fsdp", scatter_dimension=0, tiled=True)[0]

        every = lambda a: lax.all_gather(a, "seq", axis=0)
        all_down = every(r_down).reshape(k * unit_shard, D).astype(F32)
        all_up = (
            every(r_up)
            .reshape(k, shard, n, unit_shard)
            .transpose(1, 2, 0, 3)
            .reshape(shard, FF)
            .astype(F32)
        )
        all_out = every(r_out).transpose(1, 0, 2).reshape(shard, D).astype(F32)
        last = every(r_qkv)
        all_qkv = (
            last[:, :shard]
            .reshape(k, shard, 3, wide)
            .transpose(1, 2, 0, 3)
            .reshape(shard, 3 * D)
            .astype(F32)
        )
        vec = jnp.sum(last[:, shard:].astype(F32), axis=0).reshape(-1)[:count]
        piece = lambda j: vec[j * shard : (j + 1) * shard]
        return (
            jnp.stack(outs),
            jnp.stack(grad_tokens),
            all_qkv,
            piece(0),
            piece(1),
            all_out,
            piece(2),
            piece(3),
            piece(4),
            all_up,
            vec[8 * shard :],
            all_down,
            piece(5),
            piece(6),
            piece(7),
        )

    return body


def solution(mesh):
    rows = P("fsdp", "seq", None)
    matrix, vector = P("fsdp", None), P("fsdp")
    weights = (
        matrix,
        vector,
        vector,
        matrix,
        vector,
        vector,
        vector,
        matrix,
        vector,
        matrix,
        vector,
        vector,
        vector,
    )
    return jax.shard_map(
        make_body(mesh.shape["fsdp"], mesh.shape["seq"]),
        mesh=mesh,
        in_specs=(rows, P("fsdp", "seq")) + weights + (rows,),
        out_specs=(rows, rows) + weights,
        check_vma=False,
    )
```

```python
import math

import jax
import jax.numpy as jnp
from jax import lax
from jax.experimental import pallas as pl
from jax.experimental.pallas import tpu as pltpu
from jax.sharding import PartitionSpec as P

DH = 64
QBLK = 256
norm_epsilon = 1e-05
masked_score = -1e30
F32 = jnp.float32
BF16 = jnp.bfloat16
NT = (((1,), (1,)), ((), ()))
TN = (((0,), (0,)), ((), ()))
NN = (((1,), (0,)), ((), ()))


def dot(a, b, dims=NN):
    return lax.dot_general(a, b, dims, preferred_element_type=F32)


def attend_kernel(q_ref, k_ref, v_ref, seg_col, seg_row, o_ref, lse_ref):
    heads = q_ref.shape[1] // DH
    allowed = seg_col[...] == seg_row[...]
    for h in range(heads):
        cols = slice(h * DH, (h + 1) * DH)
        scores = dot(k_ref[:, cols], q_ref[:, cols], NT)
        scores = jnp.where(allowed, scores, masked_score)
        peak = jnp.max(scores, axis=0, keepdims=True)
        raw = jnp.exp(scores - peak)
        total = jnp.sum(raw, axis=0, keepdims=True)
        part = dot(v_ref[:, cols], raw.astype(BF16), TN) / total
        o_ref[:, cols] = part.T.astype(BF16)
        lse_ref[h : h + 1, :] = peak + jnp.log(total)


def attend(qkv, seg_col, seg_row):
    length, width = qkv.shape[0], qkv.shape[1] // 3
    heads = width // DH
    return pl.pallas_call(
        attend_kernel,
        grid=(length // QBLK,),
        in_specs=[
            pl.BlockSpec((QBLK, width), lambda i: (i, 0)),
            pl.BlockSpec((length, width), lambda i: (0, 1)),
            pl.BlockSpec((length, width), lambda i: (0, 2)),
            pl.BlockSpec((length, 1), lambda i: (0, 0)),
            pl.BlockSpec((1, QBLK), lambda i: (0, i)),
        ],
        out_specs=[
            pl.BlockSpec((QBLK, width), lambda i: (i, 0)),
            pl.BlockSpec((heads, QBLK), lambda i: (0, i)),
        ],
        out_shape=[
            jax.ShapeDtypeStruct((length, width), BF16),
            jax.ShapeDtypeStruct((heads, length), F32),
        ],
        compiler_params=pltpu.CompilerParams(vmem_limit_bytes=40 * 2**20),
        cost_estimate=pl.CostEstimate(
            flops=16 * heads * length * length * DH,
            bytes_accessed=8 * length * width,
            transcendentals=heads * length * length,
        ),
    )(qkv, qkv, qkv, seg_col, seg_row)


def back_kernel(q_ref, k_ref, v_ref, do_ref, lse_ref, seg_col, seg_row, out_ref, dk_acc, dv_acc):
    step = pl.program_id(0)
    width = q_ref.shape[1]
    heads = width // DH

    @pl.when(step == 0)
    def _():
        dk_acc[...] = jnp.zeros_like(dk_acc)
        dv_acc[...] = jnp.zeros_like(dv_acc)

    allowed = seg_col[...] == seg_row[...]
    rows = pl.ds(pl.multiple_of(step * QBLK, QBLK), QBLK)
    for h in range(heads):
        cols = slice(h * DH, (h + 1) * DH)
        queries, keys, grads = q_ref[:, cols], k_ref[:, cols], do_ref[:, cols]
        scores = dot(keys, queries, NT)
        soft = jnp.exp(jnp.where(allowed, scores, masked_score) - lse_ref[h : h + 1, :])
        grad_soft = dot(v_ref[:, cols], grads, NT)
        inner = jnp.sum(soft * grad_soft, axis=0, keepdims=True)
        grad_scores = (soft * (grad_soft - inner)).astype(BF16)
        dk_acc[:, cols] += dot(grad_scores, queries)
        dv_acc[:, cols] += dot(soft.astype(BF16), grads)
        grad_query = dot(keys, grad_scores, TN) * DH ** (-0.5)
        out_ref[rows, cols] = grad_query.T.astype(BF16)

    @pl.when(step == pl.num_programs(0) - 1)
    def _():
        out_ref[:, width : 2 * width] = dk_acc[...].astype(BF16)
        out_ref[:, 2 * width :] = dv_acc[...].astype(BF16)


def attend_back(qkv, grad_context, lse, seg_col, seg_row):
    length, width = qkv.shape[0], qkv.shape[1] // 3
    heads = width // DH
    return pl.pallas_call(
        back_kernel,
        grid=(length // QBLK,),
        in_specs=[
            pl.BlockSpec((QBLK, width), lambda i: (i, 0)),
            pl.BlockSpec((length, width), lambda i: (0, 1)),
            pl.BlockSpec((length, width), lambda i: (0, 2)),
            pl.BlockSpec((QBLK, width), lambda i: (i, 0)),
            pl.BlockSpec((heads, QBLK), lambda i: (0, i)),
            pl.BlockSpec((length, 1), lambda i: (0, 0)),
            pl.BlockSpec((1, QBLK), lambda i: (0, i)),
        ],
        out_specs=pl.BlockSpec((length, 3 * width), lambda i: (0, 0)),
        out_shape=jax.ShapeDtypeStruct((length, 3 * width), BF16),
        scratch_shapes=[pltpu.VMEM((length, width), F32), pltpu.VMEM((length, width), F32)],
        compiler_params=pltpu.CompilerParams(vmem_limit_bytes=40 * 2**20),
        cost_estimate=pl.CostEstimate(
            flops=40 * heads * length * length * DH,
            bytes_accessed=14 * length * width,
            transcendentals=heads * length * length,
        ),
    )(qkv, qkv, qkv, grad_context, lse, seg_col, seg_row)


def norm_rows(values):
    row_mean = jnp.mean(values, -1, keepdims=True)
    centered = values - row_mean
    inverse = lax.rsqrt(jnp.mean(centered * centered, -1, keepdims=True) + norm_epsilon)
    return centered * inverse, inverse


def norm_back(upstream, normed, inverse, gain):
    scaled = upstream * gain
    first_mean = jnp.mean(scaled, -1, keepdims=True)
    second_mean = jnp.mean(scaled * normed, -1, keepdims=True)
    return inverse * (scaled - first_mean - normed * second_mean)


def make_body(n, k):
    def swap(array, flip):
        return lax.ppermute(array, "seq", [(i, i ^ flip) for i in range(k)])

    def gather(own):
        near = swap(own, 1)
        far = swap(own, 2)
        return jnp.concatenate([own, near, far, swap(far, 1)], axis=0)

    def scatter(partial):
        rows = partial.shape[0] // k
        low = partial.astype(BF16)
        block = lambda j: low[j * rows : (j + 1) * rows]
        got = swap(jnp.concatenate([block(1), block(3)], axis=0), 1)
        exact = lambda j: partial[j * rows : (j + 1) * rows]
        other = swap((exact(2) + got[rows:].astype(F32)).astype(BF16), 2)
        return exact(0) + got[:rows].astype(F32) + other.astype(F32)

    def halve(array, order):
        me = lax.axis_index("fsdp")
        width = n.bit_length() - 1
        array = array.reshape((2,) * width + array.shape[1:])
        for bit in order:
            mine = (me >> bit) & 1
            part = lambda side: lax.dynamic_index_in_dim(array, side, width - 1 - bit)
            pairs = [(i, i ^ (1 << bit)) for i in range(n)]
            got = lax.ppermute(part(1 - mine), "fsdp", pairs)
            array = (part(mine).astype(F32) + got.astype(F32)).astype(BF16)
        return array.reshape(array.shape[width:])

    def exchange(blocks):
        me = lax.axis_index("seq")
        return [blocks(me)] + [swap(blocks(me ^ d), d) for d in range(1, k)]

    def absolute(pieces):
        me = lax.axis_index("seq")
        stacked = jnp.stack(pieces)
        return [lax.dynamic_index_in_dim(stacked, me ^ t, 0, keepdims=False) for t in range(k)]

    def body(
        tokens,
        segments,
        qkv_weight,
        query_bias,
        value_bias,
        out_weight,
        out_bias,
        first_gain,
        first_shift,
        hidden_weight,
        hidden_bias,
        down_weight,
        down_bias,
        second_gain,
        second_shift,
        cotangent,
    ):
        me = lax.axis_index("seq")
        seqs, blk, D = tokens.shape
        FF = hidden_weight.shape[1]
        wide = D // k
        units = FF // k
        shard = D // n
        unit_shard = units // n

        small = jnp.concatenate(
            [
                query_bias,
                value_bias,
                out_bias,
                first_gain,
                first_shift,
                down_bias,
                second_gain,
                second_shift,
                hidden_bias,
            ]
        )
        count = small.shape[0]
        extra = 16
        small = jnp.pad(small, (0, extra * D - count)).reshape(extra, D)
        mine = lax.dynamic_index_in_dim(
            qkv_weight.reshape(shard, 3, k, wide), me, 2, keepdims=False
        ).reshape(shard, 3 * wide)
        out_mine = lax.dynamic_slice_in_dim(out_weight, me * wide, wide, 1)
        mine = jnp.concatenate([mine, out_mine], axis=1)
        packed = lax.all_gather(jnp.concatenate([mine, small], axis=0), "fsdp", axis=0)
        w_qkv = packed[:, :shard, : 3 * wide].reshape(D, 3 * wide)
        out_columns = packed[:, :shard, 3 * wide :].reshape(D, wide)
        vectors = packed[:, shard:].reshape(n, extra * D)[:, :count].astype(F32)
        vector = lambda j: vectors[:, j * shard : (j + 1) * shard].reshape(1, D)
        (qbias, vbias, obias, gain_one, shift_one, dbias, gain_two, shift_two) = [
            vector(j) for j in range(8)
        ]
        hbias = lax.dynamic_index_in_dim(
            vectors[:, 8 * shard :].reshape(n, k, unit_shard), me, 1, keepdims=False
        ).reshape(1, units)
        own_columns = lambda v: lax.dynamic_slice_in_dim(v, me * wide, wide, 1)
        qkv_bias = jnp.concatenate(
            [own_columns(qbias), jnp.zeros((1, wide), F32), own_columns(vbias)], axis=1
        )
        qkv_scale = jnp.concatenate(
            [jnp.full((1, wide), DH ** (-0.5), F32), jnp.ones((1, 2 * wide), F32)], axis=1
        )

        w_out = jnp.concatenate(
            absolute(exchange(lambda t: lax.dynamic_slice_in_dim(out_columns, t * wide, wide, 0))),
            axis=1,
        )
        up_mine = lax.dynamic_index_in_dim(
            hidden_weight.reshape(shard, n, k, unit_shard), me, 2, keepdims=False
        ).reshape(shard, units)
        w_up = lax.all_gather(up_mine, "fsdp", axis=0, tiled=True)
        down_mine = lax.dynamic_slice_in_dim(down_weight, me * unit_shard, unit_shard, 0)
        w_down = lax.all_gather(down_mine, "fsdp", axis=0, tiled=True)

        seg_all = jnp.concatenate(
            [segments, swap(segments, 1), swap(segments, 2), swap(segments, 3)], axis=1
        )

        state = []
        for i in range(seqs):
            x = gather(tokens[i])
            seg_col, seg_row = seg_all[i][:, None], seg_all[i][None, :]
            qkv = ((dot(x, w_qkv) + qkv_bias) * qkv_scale).astype(BF16)
            context, lse = attend(qkv, seg_col, seg_row)
            state.append([x, seg_col, seg_row, qkv, context, lse, scatter(dot(context, w_out))])
        for i in range(seqs):
            attention = state[i][-1] + obias
            normed_one, inverse_one = norm_rows(tokens[i].astype(F32) + attention)
            hidden = normed_one * gain_one + shift_one
            hid = gather(hidden.astype(BF16))
            pre = dot(hid, w_up) + hbias
            cdf = 0.5 * (1.0 + lax.erf(pre * math.sqrt(0.5)))
            act = (pre * cdf).astype(BF16)
            slope = (cdf + pre * (jnp.exp(-0.5 * pre * pre) / math.sqrt(2 * math.pi))).astype(BF16)
            branch = scatter(dot(act, w_down))
            state[i] += [normed_one, inverse_one, hidden, hid, act, slope, branch]

        outs, grad_tokens = [], []
        sums = [0.0] * 6
        g_down = g_up = g_out = g_qkv = 0.0
        s_pre = s_qkv = 0.0
        grads = []
        total = lambda a: jnp.sum(a, axis=0)
        for i in range(seqs):
            normed_one, inverse_one, hidden, hid, act, slope, branch = state[i][7:]
            normed_two, inverse_two = norm_rows(hidden + branch + dbias)
            outs.append((normed_two * gain_two + shift_two).astype(BF16))
            upstream = cotangent[i].astype(F32)
            grad_two = norm_back(upstream, normed_two, inverse_two, gain_two)
            grad_branch = grad_two.astype(BF16)
            sums[3] += total(grad_branch.astype(F32))
            sums[4] += total(upstream * normed_two)
            sums[5] += total(upstream)
            gb = gather(grad_branch)
            g_down += dot(act, gb, TN)
            grad_pre = (dot(gb, w_down, NT) * slope.astype(F32)).astype(BF16)
            s_pre += total(grad_pre.astype(F32))
            g_up += dot(hid, grad_pre, TN)
            grad_hidden = grad_two + scatter(dot(grad_pre, w_up, NT))
            grads.append(grad_hidden)

        r_hidden = lax.psum_scatter(
            jnp.concatenate([g_up.astype(BF16), g_down.astype(BF16)], axis=1),
            "fsdp",
            scatter_dimension=0,
            tiled=True,
        )

        for i in range(seqs):
            x, seg_col, seg_row, qkv, context, lse = state[i][:6]
            normed_one, inverse_one = state[i][7:9]
            grad_hidden = grads[i]
            grad_one = norm_back(grad_hidden, normed_one, inverse_one, gain_one)
            grad_attention = grad_one.astype(BF16)
            sums[0] += total(grad_attention.astype(F32))
            sums[1] += total(grad_hidden * normed_one)
            sums[2] += total(grad_hidden)
            ga = gather(grad_attention)
            g_out += dot(context, ga, TN)
            grad_context = dot(ga, w_out, NT).astype(BF16)
            dqkv = attend_back(qkv, grad_context, lse, seg_col, seg_row)
            s_qkv += total(dqkv.astype(F32))
            g_qkv += dot(x, dqkv, TN)
            grad_tokens.append(grad_one + scatter(dot(dqkv, w_qkv, NT)))

        g_out = g_out.astype(BF16)
        out_rows = jnp.concatenate(
            absolute(exchange(lambda t: lax.dynamic_slice_in_dim(g_out, t * wide, wide, 1))),
            axis=0,
        )

        place = lambda v: lax.dynamic_update_slice_in_dim(
            jnp.zeros((D,), F32), v, me * wide, 0
        )
        full = [place(s_qkv[:wide]), place(s_qkv[2 * wide :])] + sums
        hidden_sum = lax.dynamic_update_slice_in_dim(
            jnp.zeros((n, k, unit_shard), F32), s_pre.reshape(n, 1, unit_shard), me, 1
        ).reshape(n, k * unit_shard)
        vector_sums = jnp.concatenate([v.reshape(n, shard) for v in full] + [hidden_sum], axis=1)
        vector_sums = jnp.pad(vector_sums, ((0, 0), (0, extra * D - count)))
        joined = jnp.concatenate(
            [
                jnp.concatenate([g_qkv.astype(BF16), out_rows], axis=1).reshape(n, shard, D),
                vector_sums.astype(BF16).reshape(n, extra, D),
            ],
            axis=1,
        )
        every = lambda a: lax.all_gather(a, "seq", axis=0)
        both, joined = lax.optimization_barrier((every(r_hidden), joined))
        bits = list(range(n.bit_length() - 1))
        r_qkv = jnp.concatenate(
            [
                halve(joined[..., : D // 2], bits),
                halve(joined[..., D // 2 :], bits[1:] + bits[:1]),
            ],
            axis=1,
        )

        all_up = (
            both[..., :units]
            .reshape(k, shard, n, unit_shard)
            .transpose(1, 2, 0, 3)
            .reshape(shard, FF)
            .astype(F32)
        )
        all_down = both[..., units:].reshape(k * unit_shard, D).astype(F32)
        last = every(r_qkv)
        all_qkv = (
            last[:, :shard, : 3 * wide]
            .reshape(k, shard, 3, wide)
            .transpose(1, 2, 0, 3)
            .reshape(shard, 3 * D)
            .astype(F32)
        )
        all_out = last[:, :shard, 3 * wide :].transpose(1, 0, 2).reshape(shard, D).astype(F32)
        vec = jnp.sum(last[:, shard:].astype(F32), axis=0).reshape(-1)[:count]
        piece = lambda j: vec[j * shard : (j + 1) * shard]
        return (
            jnp.stack(outs),
            jnp.stack(grad_tokens),
            all_qkv,
            piece(0),
            piece(1),
            all_out,
            piece(2),
            piece(3),
            piece(4),
            all_up,
            vec[8 * shard :],
            all_down,
            piece(5),
            piece(6),
            piece(7),
        )

    return body


def solution(mesh):
    rows = P("fsdp", "seq", None)
    matrix, vector = P("fsdp", None), P("fsdp")
    weights = (
        matrix,
        vector,
        vector,
        matrix,
        vector,
        vector,
        vector,
        matrix,
        vector,
        matrix,
        vector,
        vector,
        vector,
    )
    return jax.shard_map(
        make_body(mesh.shape["fsdp"], mesh.shape["seq"]),
        mesh=mesh,
        in_specs=(rows, P("fsdp", "seq")) + weights + (rows,),
        out_specs=(rows, rows) + weights,
        check_vma=False,
    )
```
